512 devices in a mesh: row: 64 (over y, z_hi, core), rep: 8 (over z_lo, x).
Axes of the slice: x: 4, y: 8, z: 8 (z_hi: 4, z_lo: 2; z = z_hi * 2 + z_lo), core: 2. Of those that a mesh axis runs over, the one named last changes fastest.
Arguments:
- features: bfloat16 [512, 128, 128], P(('row', 'rep')), may hold values from -6 to 6
- tile_values: bfloat16 [16384, 128, 128], P(('row', 'rep')), may hold values from -0.3125 to 0.3125
- tile_rows: int32 [16384], P(('row', 'rep')), may hold values from 0 to 511, as said below
- tile_cols: int32 [16384], P(('row', 'rep')), may hold values from 0 to 511, as said below
- tile_count: int32 [512], P(('row', 'rep')), may hold values from 8 to 32, as said below
- weights: bfloat16 [3, 128, 128], replicated, may hold values from -0.75 to 0.75
- biases: float32 [3, 128], replicated, may hold values from -3 to 3
Outputs:
- output: bfloat16 [512, 128, 128], P(('row', 'rep'))
The draws below stay inside these ranges and needn't reach their ends.
Inputs may be any that keep to these rules, and one draw needn't show every extreme that they name: `tile_rows`: A slot of device d = r * 8 + c has its row block in r * 8 .. (r + 1) * 8 - 1. `tile_cols`: A slot of device d = r * 8 + c has a column block j with (j) % 8 == c; within a device the column blocks never fall from slot to slot. `tile_count`: some device has all of its slots live.
All inputs are finite; a program needn't handle non-finite values.
Results may differ from the reference program's by a relative error of at most 0.015.
Values may be sent and summed in bfloat16 or wider, within the bound.
A program may use at most 64 MiB of HBM per device.

```python
import jax
import jax.numpy as jnp
from jax import lax

TB = 128
FEAT = 128
BLK_DEV = 1
TILES_DEV = 32
LAYERS = 3
NB = 512
TILES = 16384
N_ROW = 64
N_REP = 8


def draw_tile_rows(key, part):
    key = jax.random.fold_in(key, 11)
    device_total = N_ROW * N_REP
    device_ids = jnp.arange(device_total * TILES_DEV, dtype=jnp.int32) // TILES_DEV
    row_group = device_ids // N_REP
    offset_rows = jax.random.randint(key, (device_total * TILES_DEV,), 0, N_REP * BLK_DEV, dtype=jnp.int32)
    return row_group * (N_REP * BLK_DEV) + offset_rows


def draw_tile_cols(key, part):
    key = jax.random.fold_in(key, 23)
    device_total = N_ROW * N_REP
    panel_pos = jax.random.randint(key, (device_total, TILES_DEV), 0, N_ROW * BLK_DEV, dtype=jnp.int32)
    panel_pos = jnp.sort(panel_pos, axis=1)
    rep_ids = (jnp.arange(device_total, dtype=jnp.int32) % N_REP)[:, None]
    global_cols = (panel_pos // BLK_DEV * N_REP + rep_ids) * BLK_DEV + panel_pos % BLK_DEV
    return global_cols.reshape(device_total * TILES_DEV)


def draw_tile_count(key, part):
    key = jax.random.fold_in(key, 37)
    device_total = N_ROW * N_REP
    key_full, key_pick, key_light = jax.random.split(key, 3)
    full_mask = jax.random.randint(key_full, (device_total,), 0, 8, dtype=jnp.int32) == 0
    chosen = jax.random.randint(key_pick, (), 0, device_total, dtype=jnp.int32)
    full_mask = full_mask | (jnp.arange(device_total, dtype=jnp.int32) == chosen)
    light = jax.random.randint(key_light, (device_total,), TILES_DEV // 4, TILES_DEV // 2 + 1, dtype=jnp.int32)
    return jnp.where(full_mask, TILES_DEV, light).astype(jnp.int32)


def block_scale(stream_key, shape, shards, least, top_value):
    factor_of = 1.0
    for axis_at, blocks in shards:
        draws = jax.random.uniform(jax.random.fold_in(jax.random.fold_in(stream_key, 6), axis_at), (blocks,), jnp.float32, least / len(shards), top_value / len(shards))
        factor_of = factor_of * jnp.repeat(jnp.exp(draws), shape[axis_at] // blocks).reshape((-1,) + (1,) * (len(shape) - 1 - axis_at))
    return factor_of


def normal_values(key, dims, spread, reach, cuts=(), held_as=jnp.bfloat16):
    drawn = jax.random.normal(key, dims, jnp.float32) * spread
    if len(cuts) > 0:
        drawn = block_scale(key, dims, cuts, -0.22, 0.18) * drawn
    return jnp.clip(drawn, min=-reach, max=reach).astype(held_as)


def setup_inputs(seed: int = 0) -> dict:
    key_of = jax.random.split(jax.random.key(seed), 8)
    features = normal_values(key_of[0], (NB, TB, FEAT), 1.0, 6.0, ((0, 512),))
    tile_values = normal_values(key_of[1], (TILES, TB, TB), ((TB * TILES_DEV // (2 * BLK_DEV)) ** -0.5), 0.3125, ((0, 512),))
    tile_rows = draw_tile_rows(jax.random.fold_in(key_of[7], 71), 0)
    tile_cols = draw_tile_cols(jax.random.fold_in(key_of[7], 71), 0)
    tile_count = draw_tile_count(jax.random.fold_in(key_of[7], 71), 0)
    weights = normal_values(key_of[5], (LAYERS, FEAT, FEAT), (FEAT // 2) ** -0.5, 0.75)
    biases = normal_values(key_of[6], (LAYERS, FEAT), 0.5, 3.0, (), jnp.float32)
    return dict(features=features, tile_values=tile_values, tile_rows=tile_rows, tile_cols=tile_cols, tile_count=tile_count, weights=weights, biases=biases)


def reference(features, tile_values, tile_rows, tile_cols, tile_count, weights, biases):
    device_total = N_ROW * N_REP
    values_dev = tile_values.reshape(device_total, TILES_DEV, TB, TB)
    rows_dev = tile_rows.reshape(device_total, TILES_DEV)
    cols_dev = tile_cols.reshape(device_total, TILES_DEV)
    slot_ids = jnp.arange(TILES_DEV, dtype=jnp.int32)
    alive_dev = (slot_ids[None, :] < tile_count[:, None]).astype(jnp.float32)
    hidden = features
    for layer_idx in range(LAYERS):
        def one_device(totals, inputs, source=hidden):
            values, row_blocks, col_blocks, alive_mask = inputs
            picked = source[col_blocks].astype(jnp.float32)
            product = jnp.einsum("tij,tjf->tif", values.astype(jnp.float32), picked,
                                 precision=lax.Precision.HIGHEST)
            product = product * alive_mask[:, None, None]
            return totals.at[row_blocks].add(product), None

        start_sum = jnp.zeros((NB, TB, FEAT), jnp.float32)
        totals, unused = lax.scan(one_device, start_sum, (values_dev, rows_dev, cols_dev, alive_dev))
        aggregate = totals.astype(jnp.bfloat16)
        mixed_rows = jnp.einsum("bif,fg->big", aggregate.astype(jnp.float32),
                                weights[layer_idx].astype(jnp.float32),
                                precision=lax.Precision.HIGHEST) + biases[layer_idx]
        hidden = jnp.maximum(mixed_rows, 0.0).astype(jnp.bfloat16)
    return hidden
```

```python
import jax
import jax.numpy as jnp
from jax import lax
from jax.experimental import pallas as pl
from jax.experimental.pallas import tpu as pltpu
from jax.sharding import PartitionSpec as P

MESH = pl.DeviceIdType.MESH
NY, NZ, NC = 8, 4, 2
CUT = 64


def plan_kernel(rows_ref, cols_ref, count_ref, plan_ref, keep_ref, ends_ref, has_ref, fill):
    slots, groups = rows_ref.shape[0], ends_ref.shape[0]
    live = count_ref[0]

    def clear(g, _):
        fill[g] = 0
        return 0

    def count(t, _):
        g = lax.rem(rows_ref[t], groups)
        fill[g] = fill[g] + (t < live).astype(jnp.int32)
        return 0

    def offsets(g, start):
        size = fill[g]
        fill[g] = start
        ends_ref[g] = jnp.maximum(start + size - 1, 0)
        has_ref[g] = (size > 0).astype(jnp.float32)
        return start + size

    def blank(t, _):
        plan_ref[0, t] = 0
        plan_ref[1, t] = 0
        keep_ref[t] = 0.0
        return 0

    def place(t, _):
        @pl.when(t < live)
        def _():
            g = lax.rem(rows_ref[t], groups)
            at = fill[g]
            fill[g] = at + 1
            plan_ref[0, at] = t
            plan_ref[1, at] = cols_ref[t] // groups
            keep_ref[at] = jnp.where(has_ref[g] > 1.5, 1.0, 0.0)
            has_ref[g] = 2.0

        return 0

    def settle(g, _):
        has_ref[g] = jnp.minimum(has_ref[g], 1.0)
        return 0

    lax.fori_loop(0, groups, clear, 0)
    lax.fori_loop(0, slots, count, 0)
    lax.fori_loop(0, groups, offsets, 0)
    lax.fori_loop(0, slots, blank, 0)
    lax.fori_loop(0, slots, place, 0)
    lax.fori_loop(0, groups, settle, 0)


def layers_kernel(
    plan_ref, keep_ref, ends_ref, has_ref, feat_ref, tiles_hbm, weights_ref, biases_ref, out_ref,
    tiles, panel_0, panel_1, panel_2, runs, parts, inbox, hidden,
    tile_sem, z_out, z_in, y_out, y_in, a_out, a_in, b_out, b_in, s_out, s_in, r_out, r_in,
):
    slots = tiles.shape[0]
    reps = parts.shape[1]
    row, rep = lax.axis_index("row"), lax.axis_index("rep")
    core = lax.rem(row, NC)
    z = lax.rem(row // NC, NZ)
    y = row // (NC * NZ)

    def row_of(dy, dz, other=0):
        yy = lax.rem(y + dy + NY, NY)
        zz = lax.rem(z + dz + NZ, NZ)
        cc = 1 - core if other else core
        return (yy * NZ + zz) * NC + cc

    def at(dy, dz, other=0):
        return (row_of(dy, dz, other), rep)

    load = pltpu.make_async_copy(tiles_hbm, tiles, tile_sem)
    load.start()

    barrier = pltpu.get_barrier_semaphore()
    peers = [at(dy, 0) for dy in range(1, NY)] + [at(0, dz) for dz in range(1, NZ)] + [at(0, 0, 1)]
    peers += [(row, lax.rem(rep + k, reps)) for k in range(1, reps)]
    for peer in peers:
        pl.semaphore_signal(barrier, inc=1, device_id=peer, device_id_type=MESH)
    hidden[...] = feat_ref[0]
    pl.semaphore_wait(barrier, len(peers))

    def remote(src, dst, out_sem, in_sem, device):
        return pltpu.make_async_remote_copy(
            src_ref=src, dst_ref=dst, send_sem=out_sem, recv_sem=in_sem, device_id=device, device_id_type=MESH
        )

    def layer(l, panel):
        panel[row] = hidden[...]

        def z_copy(dz, src):
            ref = panel.at[src]
            return remote(ref, ref, z_out.at[l, dz - 1], z_in.at[l, dz - 1], at(0, dz))

        def y_copy(dy, src):
            ref = panel.at[src]
            return remote(ref, ref, y_out.at[l, dy - 1], y_in.at[l, dy - 1], at(dy, 0))

        def a_copy(dy, dz, src):
            ref = panel.at[src, pl.ds(0, CUT)]
            return remote(ref, ref, a_out.at[l, dz - 1, dy - 1], a_in.at[l, dz - 1, dy - 1], at(dy, 0))

        def b_copy(dy, dz, src):
            ref = panel.at[src, pl.ds(CUT, 128 - CUT)]
            return remote(ref, ref, b_out.at[l, dz - 1, dy - 1], b_in.at[l, dz - 1, dy - 1], at(0, dz))

        def s_copy(dy, dz, src):
            ref = panel.at[src]
            return remote(ref, ref, s_out.at[l, dz, dy], s_in.at[l, dz, dy], at(0, 0, 1))

        y_order = (1, 7, 2, 6, 3, 5, 4)
        z_order = (1, 3, 2)
        for k in range(7):
            y_copy(y_order[k], row).start()
            if k < 3:
                z_copy(z_order[k], row).start()
        s_copy(0, 0, row).start()
        for dz in z_order:
            src = row_of(0, -dz)
            z_copy(dz, src).wait_recv()
            for dy in y_order:
                a_copy(dy, dz, src).start()
            s_copy(0, dz, src).start()
        for dy in y_order:
            src = row_of(-dy, 0)
            y_copy(dy, src).wait_recv()
            for dz in z_order:
                b_copy(dy, dz, src).start()
            s_copy(dy, 0, src).start()
        for dz in z_order:
            for dy in y_order:
                src = row_of(-dy, -dz)
                a_copy(dy, dz, src).wait_recv()
                b_copy(dy, dz, src).wait_recv()
                s_copy(dy, dz, src).start()
        for dz in range(NZ):
            for dy in range(NY):
                s_copy(dy, dz, row_of(-dy, -dz, 1)).wait_recv()

        if l == 0:
            load.wait()

        def tile_step(p, acc):
            product = jnp.dot(
                tiles[plan_ref[0, p]], panel[plan_ref[1, p]], preferred_element_type=jnp.float32
            )
            acc = acc * keep_ref[p] + product
            runs[p] = acc
            return acc

        lax.fori_loop(0, slots, tile_step, jnp.zeros((128, 128), jnp.float32), unroll=4)

        def r_copy(k, dst):
            return remote(
                parts.at[l, k], inbox.at[l, k], r_out.at[l, k - 1], r_in.at[l, k - 1], (row, dst)
            )

        for k in range(1, reps):
            dst = lax.rem(rep + k, reps)
            parts[l, k] = (runs[ends_ref[dst]] * has_ref[dst]).astype(jnp.bfloat16)
            r_copy(k, dst).start()
        total = runs[ends_ref[rep]] * has_ref[rep]
        for k in range(1, reps):
            r_copy(k, rep).wait_recv()
            total += inbox[l, k].astype(jnp.float32)
        mixed = jnp.dot(
            total.astype(jnp.bfloat16), weights_ref[l], preferred_element_type=jnp.float32
        )
        hidden[...] = jnp.maximum(mixed + biases_ref[pl.ds(l, 1), :], 0.0).astype(jnp.bfloat16)

        for dz in range(1, NZ):
            z_copy(dz, row).wait_send()
        for dy in range(1, NY):
            y_copy(dy, row).wait_send()
        for dz in range(1, NZ):
            for dy in range(1, NY):
                a_copy(dy, dz, row).wait_send()
                b_copy(dy, dz, row).wait_send()
        for dz in range(NZ):
            for dy in range(NY):
                s_copy(dy, dz, row).wait_send()
        for k in range(1, reps):
            r_copy(k, rep).wait_send()

    for l, panel in enumerate((panel_0, panel_1, panel_2)):
        layer(l, panel)
    out_ref[0] = hidden[...]


def shards(features, tile_values, tile_rows, tile_cols, tile_count, weights, biases):
    slots = tile_values.shape[0]
    layers = weights.shape[0]
    reps = lax.axis_size("rep")
    smem = pl.BlockSpec(memory_space=pltpu.SMEM)
    vmem = pl.BlockSpec(memory_space=pltpu.VMEM)
    plan, keep, ends, has = pl.pallas_call(
        plan_kernel,
        out_shape=(
            jax.ShapeDtypeStruct((2, slots), jnp.int32),
            jax.ShapeDtypeStruct((slots,), jnp.float32),
            jax.ShapeDtypeStruct((reps,), jnp.int32),
            jax.ShapeDtypeStruct((reps,), jnp.float32),
        ),
        in_specs=[smem] * 3,
        out_specs=(smem,) * 4,
        scratch_shapes=[pltpu.SMEM((reps,), jnp.int32)],
        name="plan",
    )(tile_rows, tile_cols, tile_count)
    dma = pltpu.SemaphoreType.DMA
    return pl.pallas_call(
        layers_kernel,
        out_shape=jax.ShapeDtypeStruct(features.shape, jnp.bfloat16),
        in_specs=[smem] * 4 + [vmem, pl.BlockSpec(memory_space=pl.ANY), vmem, vmem],
        out_specs=vmem,
        scratch_shapes=[
            pltpu.VMEM((slots, 128, 128), jnp.bfloat16),
            pltpu.VMEM((NY * NZ * NC, 128, 128), jnp.bfloat16),
            pltpu.VMEM((NY * NZ * NC, 128, 128), jnp.bfloat16),
            pltpu.VMEM((NY * NZ * NC, 128, 128), jnp.bfloat16),
            pltpu.VMEM((slots, 128, 128), jnp.float32),
            pltpu.VMEM((layers, reps, 128, 128), jnp.bfloat16),
            pltpu.VMEM((layers, reps, 128, 128), jnp.bfloat16),
            pltpu.VMEM((128, 128), jnp.bfloat16),
            dma,
            dma((layers, NZ - 1)),
            dma((layers, NZ - 1)),
            dma((layers, NY - 1)),
            dma((layers, NY - 1)),
            dma((layers, NZ - 1, NY - 1)),
            dma((layers, NZ - 1, NY - 1)),
            dma((layers, NZ - 1, NY - 1)),
            dma((layers, NZ - 1, NY - 1)),
            dma((layers, NZ, NY)),
            dma((layers, NZ, NY)),
            dma((layers, reps - 1)),
            dma((layers, reps - 1)),
        ],
        compiler_params=pltpu.CompilerParams(
            collective_id=0, has_side_effects=True, vmem_limit_bytes=48 << 20
        ),
        name="layers",
    )(plan, keep, ends, has, features, tile_values, weights, biases)


def solution(mesh):
    in_specs = (
        P(("row", "rep"), None, None),
        P(("row", "rep"), None, None),
        P(("row", "rep")),
        P(("row", "rep")),
        P(("row", "rep")),
        P(),
        P(),
    )
    out_specs = P(("row", "rep"), None, None)
    return jax.shard_map(shards, mesh=mesh, in_specs=in_specs, out_specs=out_specs, check_vma=False)
```

```python
import jax
import jax.numpy as jnp
from jax import lax
from jax.experimental import pallas as pl
from jax.experimental.pallas import tpu as pltpu
from jax.sharding import PartitionSpec as P

MESH = pl.DeviceIdType.MESH
NY, NZ, NC = 8, 4, 2
GROUPS = 8
SIDE = 128
CUT = 80
HEAD = pl.ds(0, CUT)
TAIL = pl.ds(CUT, SIDE - CUT)


def layers_kernel(
    rows_hbm, cols_hbm, count_ref, feat_hbm, tiles_hbm, weights_hbm, biases_hbm, out_ref,
    rows, cols, before, ends, tiles, weights, biases, panel_0, panel_1, panel_2, runs, parts, inbox,
    load_sem, za_out, za_in, ya_out, ya_in, yb_out, yb_in, zb_out, zb_in,
    sa_out, sa_in, sb_out, sb_in, r_out, r_in,
):
    slots = tiles.shape[0]
    reps = parts.shape[1]
    row, rep = lax.axis_index("row"), lax.axis_index("rep")
    core = lax.rem(row, NC)
    z = lax.rem(row // NC, NZ)
    y = row // (NC * NZ)
    ys = [lax.rem(y + d, NY) for d in range(NY)]
    zs = [lax.rem(z + d, NZ) for d in range(NZ)]
    sibling = (row + 1 - 2 * core, rep)

    def y_peer(d):
        return ((ys[d] * NZ + z) * NC + core, rep)

    def z_peer(d):
        return ((y * NZ + zs[d]) * NC + core, rep)

    loads = [
        pltpu.make_async_copy(src, dst, load_sem.at[k])
        for k, (src, dst) in enumerate(
            (
                (feat_hbm.at[0], panel_0.at[core, y, z]),
                (rows_hbm, rows),
                (cols_hbm, cols),
                (tiles_hbm, tiles),
                (weights_hbm, weights),
                (biases_hbm, biases),
            )
        )
    ]
    for load in loads:
        load.start()

    barrier = pltpu.get_barrier_semaphore()
    peers = [y_peer(d) for d in range(1, NY)] + [z_peer(d) for d in range(1, NZ)] + [sibling]
    peers += [(row, lax.rem(rep + k, reps)) for k in range(1, reps)]
    for peer in peers:
        pl.semaphore_signal(barrier, inc=1, device_id=peer, device_id_type=MESH)
    loads[0].wait()
    pl.semaphore_wait(barrier, len(peers))

    def remote(src, dst, out_sem, in_sem, device):
        return pltpu.make_async_remote_copy(
            src_ref=src, dst_ref=dst, send_sem=out_sem, recv_sem=in_sem, device_id=device, device_id_type=MESH
        )

    def hop(d):
        return {3: 1, 5: 7}.get(d, d)

    def link_slots():
        for load in loads[1:3]:
            load.wait()
        live = count_ref[0]
        last = [jnp.int32(slots)] * GROUPS
        for t in range(slots):
            group = lax.rem(rows[t], GROUPS)
            previous = jnp.int32(slots)
            for g in range(GROUPS):
                hit = group == g
                previous = jnp.where(hit, last[g], previous)
                last[g] = jnp.where(hit & (t < live), t, last[g])
            before[t] = previous
        for g in range(GROUPS):
            ends[g] = last[g]

    def layer(l, panel):
        def za(d, src):
            ref = panel.at[core, y, src, HEAD]
            return remote(ref, ref, za_out.at[l, d], za_in.at[l, d], z_peer(d))

        def ya(d, src, part=0):
            if d == 4:
                ref = panel.at[core, src, pl.ds(2 * part, 2), HEAD]
                return remote(ref, ref, ya_out.at[l, NY * part + 4], ya_in.at[l, NY * part + 4], y_peer(6 if part else 2))
            ref = panel.at[core, src, :, HEAD]
            return remote(ref, ref, ya_out.at[l, d], ya_in.at[l, d], y_peer(hop(d)))

        def yb(d, src):
            ref = panel.at[core, src, z, TAIL]
            return remote(ref, ref, yb_out.at[l, d], yb_in.at[l, d], y_peer(2 if d == 4 else hop(d)))

        def zb(d, src):
            ref = panel.at[core, :, src, TAIL]
            return remote(ref, ref, zb_out.at[l, d], zb_in.at[l, d], z_peer(d))

        def sa(d, src, side):
            ref = panel.at[side, src, :, HEAD]
            return remote(ref, ref, sa_out.at[l, d], sa_in.at[l, d], sibling)

        def sb(d, src, side):
            ref = panel.at[side, :, src, TAIL]
            return remote(ref, ref, sb_out.at[l, d], sb_in.at[l, d], sibling)

        def back(d):
            return ys[(NY - d) % NY]

        def back_z(d):
            return zs[(NZ - d) % NZ]

        for d in (2, 6):
            yb(d, y).start()
        for d in (2, 1, 3):
            za(d, z).start()
        for d in (1, 7):
            yb(d, y).start()
        if l == 0:
            runs[...] = jnp.zeros_like(runs)
            link_slots()
        yb(2, back(2)).wait_recv()
        yb(4, back(2)).start()
        yb(3, back(2)).start()
        yb(6, back(6)).wait_recv()
        yb(5, back(6)).start()
        for d in (1, 3, 2):
            za(d, back_z(d)).wait_recv()
        for d in (2, 6, 1, 7):
            ya(d, y).start()
        sa(0, y, core).start()
        for d in (1, 7, 3, 5, 4):
            yb(d, back(d)).wait_recv()
        for d in (2, 1, 3):
            zb(d, z).start()
        sb(0, z, core).start()
        ya(2, back(2)).wait_recv()
        ya(4, back(2), 0).start()
        ya(3, back(2)).start()
        ya(6, back(6)).wait_recv()
        ya(4, back(6), 1).start()
        ya(5, back(6)).start()
        sa(2, back(2), core).start()
        sa(6, back(6), core).start()
        for d in (1, 7):
            ya(d, back(d)).wait_recv()
            sa(d, back(d), core).start()
        for d in (1, 3, 2):
            zb(d, back_z(d)).wait_recv()
            sb(d, back_z(d), core).start()
        for d in (3, 5):
            ya(d, back(d)).wait_recv()
            sa(d, back(d), core).start()
        for part in range(2):
            ya(4, back(4), part).wait_recv()
        sa(4, back(4), core).start()
        for d in range(NY):
            sa(d, back(d), 1 - core).wait_recv()
        for d in range(NZ):
            sb(d, back_z(d), 1 - core).wait_recv()

        if l == 0:
            for load in loads[3:]:
                load.wait()

        def tile_step(t, _):
            at = cols[t] // GROUPS
            block = panel[lax.rem(at, NC), at // (NC * NZ), lax.rem(at // NC, NZ)]
            product = jnp.dot(tiles[t], block, preferred_element_type=jnp.float32)
            runs[t] = runs[before[t]] + product
            return 0

        lax.fori_loop(0, slots, tile_step, 0, unroll=4)

        def r_copy(k, dst):
            return remote(
                parts.at[l, k], inbox.at[l, k], r_out.at[l, k], r_in.at[l, k], (row, dst)
            )

        for k in range(1, reps):
            dst = lax.rem(rep + k, reps)
            parts[l, k] = runs[ends[dst]].astype(jnp.bfloat16)
            r_copy(k, dst).start()
        for d in range(1, NY):
            yb(d, y).wait_send()
            if d != 4:
                ya(d, y).wait_send()
        for part in range(2):
            ya(4, y, part).wait_send()
        for d in range(1, NZ):
            za(d, z).wait_send()
            zb(d, z).wait_send()
        for d in range(NY):
            sa(d, y, core).wait_send()
        for d in range(NZ):
            sb(d, z, core).wait_send()
        total = runs[ends[rep]]
        for k in range(1, reps):
            r_copy(k, rep).wait_recv()
            total += inbox[l, k].astype(jnp.float32)
        mixed = jnp.dot(
            total.astype(jnp.bfloat16), weights[l], preferred_element_type=jnp.float32
        )
        return jnp.maximum(mixed + biases[pl.ds(l, 1), :], 0.0).astype(jnp.bfloat16)

    panels = (panel_0, panel_1, panel_2)
    for l, panel in enumerate(panels):
        result = layer(l, panel)
        if l + 1 < len(panels):
            panels[l + 1][core, y, z] = result
        else:
            out_ref[0] = result
    for l in range(len(panels)):
        for k in range(1, reps):
            remote(parts.at[l, k], inbox.at[l, k], r_out.at[l, k], r_in.at[l, k], sibling).wait_send()


def shards(features, tile_values, tile_rows, tile_cols, tile_count, weights, biases):
    slots = tile_values.shape[0]
    layers = weights.shape[0]
    reps = lax.axis_size("rep")
    smem = pl.BlockSpec(memory_space=pltpu.SMEM)
    hbm = pl.BlockSpec(memory_space=pl.ANY)
    dma = pltpu.SemaphoreType.DMA
    panel = pltpu.VMEM((NC, NY, NZ, SIDE, SIDE), jnp.bfloat16)
    return pl.pallas_call(
        layers_kernel,
        out_shape=jax.ShapeDtypeStruct(features.shape, jnp.bfloat16),
        in_specs=[hbm, hbm, smem, hbm, hbm, hbm, hbm],
        out_specs=pl.BlockSpec(memory_space=pltpu.VMEM),
        scratch_shapes=[
            pltpu.SMEM((slots,), jnp.int32),
            pltpu.SMEM((slots,), jnp.int32),
            pltpu.SMEM((slots,), jnp.int32),
            pltpu.SMEM((GROUPS,), jnp.int32),
            pltpu.VMEM((slots, SIDE, SIDE), jnp.bfloat16),
            pltpu.VMEM(weights.shape, jnp.bfloat16),
            pltpu.VMEM(biases.shape, jnp.float32),
            panel,
            panel,
            panel,
            pltpu.VMEM((slots + 1, SIDE, SIDE), jnp.float32),
            pltpu.VMEM((layers, reps, SIDE, SIDE), jnp.bfloat16),
            pltpu.VMEM((layers, reps, SIDE, SIDE), jnp.bfloat16),
            dma((6,)),
            dma((layers, NZ)),
            dma((layers, NZ)),
            dma((layers, 2 * NY)),
            dma((layers, 2 * NY)),
            dma((layers, NY)),
            dma((layers, NY)),
            dma((layers, NZ)),
            dma((layers, NZ)),
            dma((layers, NY)),
            dma((layers, NY)),
            dma((layers, NZ)),
            dma((layers, NZ)),
            dma((layers, reps)),
            dma((layers, reps)),
        ],
        compiler_params=pltpu.CompilerParams(
            collective_id=0, has_side_effects=True, vmem_limit_bytes=62 << 20
        ),
        name="layers",
    )(tile_rows, tile_cols, tile_count, features, tile_values, weights, biases)


def solution(mesh):
    in_specs = (
        P(("row", "rep"), None, None),
        P(("row", "rep"), None, None),
        P(("row", "rep")),
        P(("row", "rep")),
        P(("row", "rep")),
        P(),
        P(),
    )
    out_specs = P(("row", "rep"), None, None)
    return jax.shard_map(shards, mesh=mesh, in_specs=in_specs, out_specs=out_specs, check_vma=False)
```

```python
import jax
import jax.numpy as jnp
from jax import lax
from jax.experimental import pallas as pl
from jax.experimental.pallas import tpu as pltpu
from jax.sharding import PartitionSpec as P

MESH = pl.DeviceIdType.MESH
NY, NZ, NC = 8, 4, 2
GROUPS = 8
SIDE = 128
ROWS = (pl.ds(0, SIDE),)
ALONG_Y = {(1, 1), (1, 2), (1, 3), (7, 1), (7, 2), (7, 3), (2, 2), (6, 2), (3, 2), (5, 2), (4, 2)}
OWN_ORDER = (
    ("y", 1), ("y", 7), ("z", 1), ("z", 3), ("y", 2), ("y", 6), ("z", 2), ("y", 3), ("y", 5), ("y", 4)
)
ARRIVAL_ORDER = (
    ("z", 1), ("z", 3), ("y", 1), ("y", 7), ("y", 2), ("y", 6), ("z", 2), ("y", 3), ("y", 5), ("y", 4)
)
LAST_ORDER = (
    (1, 1), (7, 1), (1, 3), (7, 3), (2, 1), (2, 3), (6, 1), (6, 3), (1, 2), (7, 2), (2, 2), (6, 2),
    (3, 1), (3, 3), (5, 1), (5, 3), (3, 2), (5, 2), (4, 1), (4, 3), (4, 2)
)


def layers_kernel(
    rows_hbm, cols_hbm, count_ref, feat_hbm, tiles_hbm, weights_hbm, biases_hbm, out_ref,
    rows, cols, place, before, ends, tiles, weights, biases, panel_0, panel_1, panel_2, runs, parts, inbox,
    load_sem, zo_out, zo_in, yo_out, yo_in, on_out, on_in, so_out, so_in, s_out, s_in, r_out, r_in,
):
    slots = tiles.shape[0]
    reps = parts.shape[1]
    panels = (panel_0, panel_1, panel_2)
    row, rep = lax.axis_index("row"), lax.axis_index("rep")
    core = lax.rem(row, NC)
    z = lax.rem(row // NC, NZ)
    y = row // (NC * NZ)
    ys = [lax.rem(y + d, NY) for d in range(NY)]
    zs = [lax.rem(z + d, NZ) for d in range(NZ)]
    sibling = (row + 1 - 2 * core, rep)

    def y_peer(d):
        return ((ys[d] * NZ + z) * NC + core, rep)

    def z_peer(d):
        return ((y * NZ + zs[d]) * NC + core, rep)

    loads = [
        pltpu.make_async_copy(src, dst, load_sem.at[k])
        for k, (src, dst) in enumerate(
            (
                (feat_hbm.at[0], panel_0.at[core, y, z]),
                (rows_hbm, rows),
                (cols_hbm, cols),
                (tiles_hbm, tiles),
                (weights_hbm, weights),
                (biases_hbm, biases),
            )
        )
    ]
    for load in loads:
        load.start()

    barrier = pltpu.get_barrier_semaphore()
    peers = [y_peer(d) for d in range(1, NY)] + [z_peer(d) for d in range(1, NZ)] + [sibling]
    peers += [(row, lax.rem(rep + k, reps)) for k in range(1, reps)]
    for peer in peers:
        pl.semaphore_signal(barrier, inc=1, device_id=peer, device_id_type=MESH)
    loads[0].wait()
    pl.semaphore_wait(barrier, len(peers))

    def remote(src, dst, out_sem, in_sem, device):
        return pltpu.make_async_remote_copy(
            src_ref=src, dst_ref=dst, send_sem=out_sem, recv_sem=in_sem, device_id=device, device_id_type=MESH
        )

    def link_slots():
        for load in loads[1:3]:
            load.wait()
        live = count_ref[0]
        last = [jnp.int32(slots)] * GROUPS
        for t in range(slots):
            group = lax.rem(rows[t], GROUPS)
            previous = jnp.int32(slots)
            for g in range(GROUPS):
                hit = group == g
                previous = jnp.where(hit, last[g], previous)
                last[g] = jnp.where(hit & (t < live), t, last[g])
            before[t] = previous
            at = cols[t] // GROUPS
            place[0, t] = lax.rem(at, NC)
            place[1, t] = at // (NC * NZ)
            place[2, t] = lax.rem(at // NC, NZ)
        for g in range(GROUPS):
            ends[g] = last[g]

    def back(d):
        return ys[(NY - d) % NY]

    def back_z(d):
        return zs[(NZ - d) % NZ]

    def zo(l, h, d, src):
        ref = panels[l].at[core, y, src, ROWS[h]]
        return remote(ref, ref, zo_out.at[l, h, d], zo_in.at[l, h, d], z_peer(d))

    def yo(l, h, d, src):
        ref = panels[l].at[core, src, z, ROWS[h]]
        return remote(ref, ref, yo_out.at[l, h, d], yo_in.at[l, h, d], y_peer(d))

    def so(l, h, side):
        ref = panels[l].at[side, y, z, ROWS[h]]
        return remote(ref, ref, so_out.at[l, h], so_in.at[l, h], sibling)

    def on(l, h, d, src, dz, src_z):
        ref = panels[l].at[core, src, src_z, ROWS[h]]
        peer = y_peer(d) if (d, dz) in ALONG_Y else z_peer(dz)
        return remote(ref, ref, on_out.at[l, h, dz, d], on_in.at[l, h, dz, d], peer)

    def sib(l, d, src, dz, src_z, side):
        ref = panels[l].at[side, src, src_z]
        return remote(ref, ref, s_out.at[l, dz, d], s_in.at[l, dz, d], sibling)

    def part(l, k, dst):
        src, to = parts.at[l, k], inbox.at[l, k]
        return remote(src, to, r_out.at[l, k], r_in.at[l, k], (row, dst))

    def send_own(l, h):
        for axis, d in OWN_ORDER:
            (yo(l, h, d, y) if axis == "y" else zo(l, h, d, z)).start()
        so(l, h, core).start()

    def gather(l):
        def y_arrival(d, h):
            yo(l, h, d, back(d)).wait_recv()
            for dz in (2, 1, 3):
                if (d, dz) not in ALONG_Y:
                    on(l, h, d, back(d), dz, z).start()
            if h == len(ROWS) - 1:
                sib(l, d, back(d), 0, z, core).start()

        def z_arrival(dz, h):
            zo(l, h, dz, back_z(dz)).wait_recv()
            for d in (4, 3, 5, 2, 6, 1, 7):
                if (d, dz) in ALONG_Y:
                    on(l, h, d, y, dz, back_z(dz)).start()
            if h == len(ROWS) - 1:
                sib(l, 0, y, dz, back_z(dz), core).start()

        for h in range(len(ROWS)):
            for axis, d in ARRIVAL_ORDER:
                (y_arrival if axis == "y" else z_arrival)(d, h)
        for d, dz in LAST_ORDER:
            for h in range(len(ROWS)):
                on(l, h, d, back(d), dz, back_z(dz)).wait_recv()
            sib(l, d, back(d), dz, back_z(dz), core).start()
        for h in range(len(ROWS)):
            so(l, h, 1 - core).wait_recv()
        for dz in range(NZ):
            for d in range(NY):
                if d or dz:
                    sib(l, d, back(d), dz, back_z(dz), 1 - core).wait_recv()

    def gather_sent(l):
        for h in range(len(ROWS)):
            so(l, h, core).wait_send()
            for d in range(1, NY):
                yo(l, h, d, y).wait_send()
            for dz in range(1, NZ):
                zo(l, h, dz, z).wait_send()
        for dz in range(NZ):
            for d in range(NY):
                if d and dz:
                    for h in range(len(ROWS)):
                        on(l, h, d, y, dz, z).wait_send()
                if d or dz:
                    sib(l, d, y, dz, z, core).wait_send()

    def products(l):
        def tile_step(t, _):
            block = panels[l][place[0, t], place[1, t], place[2, t]]
            product = jnp.dot(tiles[t], block, preferred_element_type=jnp.float32)
            runs[t] = runs[before[t]] + product
            return 0

        lax.fori_loop(0, slots, tile_step, 0, unroll=16)
        for k in range(1, reps):
            dst = lax.rem(rep + k, reps)
            parts[l, k] = runs[ends[dst]].astype(jnp.bfloat16)
            part(l, k, dst).start()

    def mix(l):
        total = runs[ends[rep]]
        for k in range(1, reps):
            part(l, k, rep).wait_recv()
            total += inbox[l, k].astype(jnp.float32)
        mixed = jnp.dot(
            total.astype(jnp.bfloat16), weights[l], preferred_element_type=jnp.float32
        )
        return jnp.maximum(mixed + biases[pl.ds(l, 1), :], 0.0).astype(jnp.bfloat16)

    layers = len(panels)
    for h in range(len(ROWS)):
        send_own(0, h)
    runs[...] = jnp.zeros_like(runs)
    link_slots()
    for l in range(layers):
        gather(l)
        if l == 0:
            for load in loads[3:]:
                load.wait()
        products(l)
        gather_sent(l)
        result = mix(l)
        if l + 1 < layers:
            panels[l + 1][core, y, z] = result
            for h in range(len(ROWS)):
                send_own(l + 1, h)
        else:
            out_ref[0] = result
    for l in range(layers):
        for k in range(1, reps):
            part(l, k, rep).wait_send()


def shards(features, tile_values, tile_rows, tile_cols, tile_count, weights, biases):
    slots = tile_values.shape[0]
    layers = weights.shape[0]
    reps = lax.axis_size("rep")
    smem = pl.BlockSpec(memory_space=pltpu.SMEM)
    hbm = pl.BlockSpec(memory_space=pl.ANY)
    dma = pltpu.SemaphoreType.DMA
    panel = pltpu.VMEM((NC, NY, NZ, SIDE, SIDE), jnp.bfloat16)
    return pl.pallas_call(
        layers_kernel,
        out_shape=jax.ShapeDtypeStruct(features.shape, jnp.bfloat16),
        in_specs=[hbm, hbm, smem, hbm, hbm, hbm, hbm],
        out_specs=pl.BlockSpec(memory_space=pltpu.VMEM),
        scratch_shapes=[
            pltpu.SMEM((slots,), jnp.int32),
            pltpu.SMEM((slots,), jnp.int32),
            pltpu.SMEM((3, slots), jnp.int32),
            pltpu.SMEM((slots,), jnp.int32),
            pltpu.SMEM((GROUPS,), jnp.int32),
            pltpu.VMEM((slots, SIDE, SIDE), jnp.bfloat16),
            pltpu.VMEM(weights.shape, jnp.bfloat16),
            pltpu.VMEM(biases.shape, jnp.float32),
            panel,
            panel,
            panel,
            pltpu.VMEM((slots + 1, SIDE, SIDE), jnp.float32),
            pltpu.VMEM((layers, reps, SIDE, SIDE), jnp.bfloat16),
            pltpu.VMEM((layers, reps, SIDE, SIDE), jnp.bfloat16),
            dma((6,)),
            dma((layers, len(ROWS), NZ)),
            dma((layers, len(ROWS), NZ)),
            dma((layers, len(ROWS), NY)),
            dma((layers, len(ROWS), NY)),
            dma((layers, len(ROWS), NZ, NY)),
            dma((layers, len(ROWS), NZ, NY)),
            dma((layers, len(ROWS))),
            dma((layers, len(ROWS))),
            dma((layers, NZ, NY)),
            dma((layers, NZ, NY)),
            dma((layers, reps)),
            dma((layers, reps)),
        ],
        compiler_params=pltpu.CompilerParams(
            collective_id=0, has_side_effects=True, vmem_limit_bytes=62 << 20
        ),
        name="layers",
    )(tile_rows, tile_cols, tile_count, features, tile_values, weights, biases)


def solution(mesh):
    in_specs = (
        P(("row", "rep"), None, None),
        P(("row", "rep"), None, None),
        P(("row", "rep")),
        P(("row", "rep")),
        P(("row", "rep")),
        P(),
        P(),
    )
    out_specs = P(("row", "rep"), None, None)
    return jax.shard_map(shards, mesh=mesh, in_specs=in_specs, out_specs=out_specs, check_vma=False)
```

```python
import jax
import jax.numpy as jnp
from jax import lax
from jax.experimental import pallas as pl
from jax.experimental.pallas import tpu as pltpu
from jax.sharding import PartitionSpec as P

MESH = pl.DeviceIdType.MESH
NY, NZ, NC = 8, 4, 2
GROUPS = 8
SIDE = 128
ROWS = (pl.ds(0, SIDE),)
ALONG_Y = {(1, 1), (1, 2), (1, 3), (7, 1), (7, 2), (7, 3), (2, 2), (6, 2), (3, 2), (5, 2), (4, 2)}
OWN_ORDER = (
    ("y", 1), ("y", 7), ("z", 1), ("z", 3), ("y", 2), ("y", 6), ("z", 2), ("y", 3), ("y", 5), ("y", 4)
)
ARRIVAL_ORDER = (
    ("z", 1), ("z", 3), ("y", 1), ("y", 7), ("y", 2), ("y", 6), ("z", 2), ("y", 3), ("y", 5), ("y", 4)
)
LAST_ORDER = (
    (1, 1), (7, 1), (1, 3), (7, 3), (2, 1), (2, 3), (6, 1), (6, 3), (1, 2), (7, 2), (2, 2), (6, 2),
    (3, 1), (3, 3), (5, 1), (5, 3), (3, 2), (5, 2), (4, 1), (4, 3), (4, 2)
)


def layers_kernel(
    rows_hbm, cols_hbm, count_ref, feat_hbm, tiles_hbm, weights_hbm, biases_hbm, out_ref,
    rows, cols, place, before, ends, tiles, weights, biases, panel_0, panel_1, panel_2, runs, parts, inbox,
    load_sem, zo_out, zo_in, yo_out, yo_in, on_out, on_in, so_out, so_in, s_out, s_in, r_out, r_in,
):
    slots = tiles.shape[0]
    reps = parts.shape[1]
    panels = (panel_0, panel_1, panel_2)
    row, rep = lax.axis_index("row"), lax.axis_index("rep")
    core = lax.rem(row, NC)
    z = lax.rem(row // NC, NZ)
    y = row // (NC * NZ)
    ys = [lax.rem(y + d, NY) for d in range(NY)]
    zs = [lax.rem(z + d, NZ) for d in range(NZ)]
    sibling = (row + 1 - 2 * core, rep)

    def y_peer(d):
        return ((ys[d] * NZ + z) * NC + core, rep)

    def z_peer(d):
        return ((y * NZ + zs[d]) * NC + core, rep)

    loads = [
        pltpu.make_async_copy(src, dst, load_sem.at[k])
        for k, (src, dst) in enumerate(
            (
                (feat_hbm.at[0], panel_0.at[core, y, z]),
                (rows_hbm, rows),
                (cols_hbm, cols),
                (tiles_hbm, tiles),
                (weights_hbm, weights),
                (biases_hbm, biases),
            )
        )
    ]
    for load in loads:
        load.start()

    barrier = pltpu.get_barrier_semaphore()
    peers = [y_peer(d) for d in range(1, NY)] + [z_peer(d) for d in range(1, NZ)] + [sibling]
    peers += [(row, lax.rem(rep + k, reps)) for k in range(1, reps)]
    for peer in peers:
        pl.semaphore_signal(barrier, inc=1, device_id=peer, device_id_type=MESH)
    loads[0].wait()
    pl.semaphore_wait(barrier, len(peers))

    def remote(src, dst, out_sem, in_sem, device):
        return pltpu.make_async_remote_copy(
            src_ref=src, dst_ref=dst, send_sem=out_sem, recv_sem=in_sem, device_id=device, device_id_type=MESH
        )

    def link_slots():
        for load in loads[1:3]:
            load.wait()
        live = count_ref[0]
        last = [jnp.int32(slots)] * GROUPS
        for t in range(slots):
            group = lax.rem(rows[t], GROUPS)
            previous = jnp.int32(slots)
            for g in range(GROUPS):
                hit = group == g
                previous = jnp.where(hit, last[g], previous)
                last[g] = jnp.where(hit & (t < live), t, last[g])
            before[t] = previous
            at = cols[t] // GROUPS
            place[0, t] = lax.rem(at, NC)
            place[1, t] = at // (NC * NZ)
            place[2, t] = lax.rem(at // NC, NZ)
        for g in range(GROUPS):
            ends[g] = last[g]

    def back(d):
        return ys[(NY - d) % NY]

    def back_z(d):
        return zs[(NZ - d) % NZ]

    def zo(l, h, d, src):
        ref = panels[l].at[core, y, src, ROWS[h]]
        return remote(ref, ref, zo_out.at[l, h, d], zo_in.at[l, h, d], z_peer(d))

    def yo(l, h, d, src):
        ref = panels[l].at[core, src, z, ROWS[h]]
        return remote(ref, ref, yo_out.at[l, h, d], yo_in.at[l, h, d], y_peer(d))

    def so(l, h, side):
        ref = panels[l].at[side, y, z, ROWS[h]]
        return remote(ref, ref, so_out.at[l, h], so_in.at[l, h], sibling)

    def on(l, h, d, src, dz, src_z):
        ref = panels[l].at[core, src, src_z, ROWS[h]]
        peer = y_peer(d) if (d, dz) in ALONG_Y else z_peer(dz)
        return remote(ref, ref, on_out.at[l, h, dz, d], on_in.at[l, h, dz, d], peer)

    def sib(l, d, src, dz, src_z, side):
        ref = panels[l].at[side, src, src_z]
        return remote(ref, ref, s_out.at[l, dz, d], s_in.at[l, dz, d], sibling)

    def part(l, k, dst):
        src, to = parts.at[l, k], inbox.at[l, k]
        return remote(src, to, r_out.at[l, k], r_in.at[l, k], (row, dst))

    def send_own(l, h):
        for axis, d in OWN_ORDER:
            (yo(l, h, d, y) if axis == "y" else zo(l, h, d, z)).start()
        so(l, h, core).start()

    def gather(l):
        def y_arrival(d, h):
            yo(l, h, d, back(d)).wait_recv()
            for dz in (1, 3, 2):
                if (d, dz) not in ALONG_Y:
                    on(l, h, d, back(d), dz, z).start()
            if h == len(ROWS) - 1:
                sib(l, d, back(d), 0, z, core).start()

        def z_arrival(dz, h):
            zo(l, h, dz, back_z(dz)).wait_recv()
            for d in (1, 7, 2, 6, 3, 5, 4):
                if (d, dz) in ALONG_Y:
                    on(l, h, d, y, dz, back_z(dz)).start()
            if h == len(ROWS) - 1:
                sib(l, 0, y, dz, back_z(dz), core).start()

        for h in range(len(ROWS)):
            for axis, d in ARRIVAL_ORDER:
                (y_arrival if axis == "y" else z_arrival)(d, h)
        for d, dz in LAST_ORDER:
            for h in range(len(ROWS)):
                on(l, h, d, back(d), dz, back_z(dz)).wait_recv()
            sib(l, d, back(d), dz, back_z(dz), core).start()
        for h in range(len(ROWS)):
            so(l, h, 1 - core).wait_recv()
        for dz in range(NZ):
            for d in range(NY):
                if d or dz:
                    sib(l, d, back(d), dz, back_z(dz), 1 - core).wait_recv()

    def gather_sent(l):
        for h in range(len(ROWS)):
            so(l, h, core).wait_send()
            for d in range(1, NY):
                yo(l, h, d, y).wait_send()
            for dz in range(1, NZ):
                zo(l, h, dz, z).wait_send()
        for dz in range(NZ):
            for d in range(NY):
                if d and dz:
                    for h in range(len(ROWS)):
                        on(l, h, d, y, dz, z).wait_send()
                if d or dz:
                    sib(l, d, y, dz, z, core).wait_send()

    def products(l):
        def tile_step(t, _):
            block = panels[l][place[0, t], place[1, t], place[2, t]]
            product = jnp.dot(tiles[t], block, preferred_element_type=jnp.float32)
            runs[t] = runs[before[t]] + product
            return 0

        lax.fori_loop(0, slots, tile_step, 0, unroll=16)
        for k in range(1, reps):
            dst = lax.rem(rep + k, reps)
            parts[l, k] = runs[ends[dst]].astype(jnp.bfloat16)
            part(l, k, dst).start()

    def mix(l):
        total = runs[ends[rep]]
        for k in range(1, reps):
            part(l, k, rep).wait_recv()
            total += inbox[l, k].astype(jnp.float32)
        mixed = jnp.dot(
            total.astype(jnp.bfloat16), weights[l], preferred_element_type=jnp.float32
        )
        return jnp.maximum(mixed + biases[pl.ds(l, 1), :], 0.0).astype(jnp.bfloat16)

    layers = len(panels)
    for h in range(len(ROWS)):
        send_own(0, h)
    runs[...] = jnp.zeros_like(runs)
    link_slots()
    for l in range(layers):
        gather(l)
        if l == 0:
            for load in loads[3:]:
                load.wait()
        products(l)
        gather_sent(l)
        result = mix(l)
        if l + 1 < layers:
            panels[l + 1][core, y, z] = result
            for h in range(len(ROWS)):
                send_own(l + 1, h)
        else:
            out_ref[0] = result
    for l in range(layers):
        for k in range(1, reps):
            part(l, k, rep).wait_send()


def shards(features, tile_values, tile_rows, tile_cols, tile_count, weights, biases):
    slots = tile_values.shape[0]
    layers = weights.shape[0]
    reps = lax.axis_size("rep")
    smem = pl.BlockSpec(memory_space=pltpu.SMEM)
    hbm = pl.BlockSpec(memory_space=pl.ANY)
    dma = pltpu.SemaphoreType.DMA
    panel = pltpu.VMEM((NC, NY, NZ, SIDE, SIDE), jnp.bfloat16)
    return pl.pallas_call(
        layers_kernel,
        out_shape=jax.ShapeDtypeStruct(features.shape, jnp.bfloat16),
        in_specs=[hbm, hbm, smem, hbm, hbm, hbm, hbm],
        out_specs=pl.BlockSpec(memory_space=pltpu.VMEM),
        scratch_shapes=[
            pltpu.SMEM((slots,), jnp.int32),
            pltpu.SMEM((slots,), jnp.int32),
            pltpu.SMEM((3, slots), jnp.int32),
            pltpu.SMEM((slots,), jnp.int32),
            pltpu.SMEM((GROUPS,), jnp.int32),
            pltpu.VMEM((slots, SIDE, SIDE), jnp.bfloat16),
            pltpu.VMEM(weights.shape, jnp.bfloat16),
            pltpu.VMEM(biases.shape, jnp.float32),
            panel,
            panel,
            panel,
            pltpu.VMEM((slots + 1, SIDE, SIDE), jnp.float32),
            pltpu.VMEM((layers, reps, SIDE, SIDE), jnp.bfloat16),
            pltpu.VMEM((layers, reps, SIDE, SIDE), jnp.bfloat16),
            dma((6,)),
            dma((layers, len(ROWS), NZ)),
            dma((layers, len(ROWS), NZ)),
            dma((layers, len(ROWS), NY)),
            dma((layers, len(ROWS), NY)),
            dma((layers, len(ROWS), NZ, NY)),
            dma((layers, len(ROWS), NZ, NY)),
            dma((layers, len(ROWS))),
            dma((layers, len(ROWS))),
            dma((layers, NZ, NY)),
            dma((layers, NZ, NY)),
            dma((layers, reps)),
            dma((layers, reps)),
        ],
        compiler_params=pltpu.CompilerParams(
            collective_id=0, has_side_effects=True, vmem_limit_bytes=62 << 20
        ),
        name="layers",
    )(tile_rows, tile_cols, tile_count, features, tile_values, weights, biases)


def solution(mesh):
    in_specs = (
        P(("row", "rep"), None, None),
        P(("row", "rep"), None, None),
        P(("row", "rep")),
        P(("row", "rep")),
        P(("row", "rep")),
        P(),
        P(),
    )
    out_specs = P(("row", "rep"), None, None)
    return jax.shard_map(shards, mesh=mesh, in_specs=in_specs, out_specs=out_specs, check_vma=False)
```

```python
import jax
import jax.numpy as jnp
from jax import lax
from jax.experimental import pallas as pl
from jax.experimental.pallas import tpu as pltpu
from jax.sharding import PartitionSpec as P

MESH = pl.DeviceIdType.MESH
NY, NZ, NC = 8, 4, 2
GROUPS = 8
SIDE = 128
ROWS = (pl.ds(0, SIDE),)
ALONG_Y = {(1, 1), (1, 2), (1, 3), (7, 1), (7, 2), (7, 3), (2, 2), (6, 2), (3, 2), (5, 2), (4, 2)}
OWN_ORDER = (
    ("y", 1), ("y", 7), ("z", 1), ("z", 3), ("y", 2), ("y", 6), ("z", 2), ("y", 3), ("y", 5), ("y", 4)
)
ARRIVAL_ORDER = (
    ("z", 1), ("z", 3), ("y", 1), ("y", 7), ("y", 2), ("y", 6), ("z", 2), ("y", 3), ("y", 5), ("y", 4)
)
LAST_ORDER = (
    (1, 1), (7, 1), (1, 3), (7, 3), (2, 1), (2, 3), (6, 1), (6, 3), (1, 2), (7, 2), (2, 2), (6, 2),
    (3, 1), (3, 3), (5, 1), (5, 3), (3, 2), (5, 2), (4, 1), (4, 3), (4, 2)
)


def layers_kernel(
    rows_hbm, cols_hbm, count_ref, feat_hbm, tiles_hbm, weights_hbm, biases_hbm, out_ref,
    rows, cols, place, before, ends, tiles, weights, biases, panel_0, panel_1, panel_2, runs, parts, inbox,
    load_sem, zo_out, zo_in, yo_out, yo_in, on_out, on_in, so_out, so_in, s_out, s_in, r_out, r_in,
):
    slots = tiles.shape[0]
    reps = parts.shape[1]
    panels = (panel_0, panel_1, panel_2)
    row, rep = lax.axis_index("row"), lax.axis_index("rep")
    core = lax.rem(row, NC)
    z = lax.rem(row // NC, NZ)
    y = row // (NC * NZ)
    ys = [lax.rem(y + d, NY) for d in range(NY)]
    zs = [lax.rem(z + d, NZ) for d in range(NZ)]
    sibling = (row + 1 - 2 * core, rep)

    def y_peer(d):
        return ((ys[d] * NZ + z) * NC + core, rep)

    def z_peer(d):
        return ((y * NZ + zs[d]) * NC + core, rep)

    loads = [
        pltpu.make_async_copy(src, dst, load_sem.at[k])
        for k, (src, dst) in enumerate(
            (
                (feat_hbm.at[0], panel_0.at[core, y, z]),
                (rows_hbm, rows),
                (cols_hbm, cols),
                (tiles_hbm, tiles),
                (weights_hbm, weights),
                (biases_hbm, biases),
            )
        )
    ]
    for load in loads:
        load.start()

    barrier = pltpu.get_barrier_semaphore()
    peers = [y_peer(d) for d in range(1, NY)] + [z_peer(d) for d in range(1, NZ)] + [sibling]
    peers += [(row, lax.rem(rep + k, reps)) for k in range(1, reps)]
    for peer in peers:
        pl.semaphore_signal(barrier, inc=1, device_id=peer, device_id_type=MESH)
    loads[0].wait()
    pl.semaphore_wait(barrier, len(peers))

    def remote(src, dst, out_sem, in_sem, device):
        return pltpu.make_async_remote_copy(
            src_ref=src, dst_ref=dst, send_sem=out_sem, recv_sem=in_sem, device_id=device, device_id_type=MESH
        )

    def link_slots():
        for load in loads[1:3]:
            load.wait()
        live = count_ref[0]
        last = [jnp.int32(slots)] * GROUPS
        for t in range(slots):
            group = lax.rem(rows[t], GROUPS)
            previous = jnp.int32(slots)
            for g in range(GROUPS):
                hit = group == g
                previous = jnp.where(hit, last[g], previous)
                last[g] = jnp.where(hit & (t < live), t, last[g])
            before[t] = previous
            at = cols[t] // GROUPS
            place[0, t] = lax.rem(at, NC)
            place[1, t] = at // (NC * NZ)
            place[2, t] = lax.rem(at // NC, NZ)
        for g in range(GROUPS):
            ends[g] = last[g]

    def back(d):
        return ys[(NY - d) % NY]

    def back_z(d):
        return zs[(NZ - d) % NZ]

    def zo(l, h, d, src):
        ref = panels[l].at[core, y, src, ROWS[h]]
        return remote(ref, ref, zo_out.at[l, h, d], zo_in.at[l, h, d], z_peer(d))

    def yo(l, h, d, src):
        ref = panels[l].at[core, src, z, ROWS[h]]
        return remote(ref, ref, yo_out.at[l, h, d], yo_in.at[l, h, d], y_peer(d))

    def so(l, h, side):
        ref = panels[l].at[side, y, z, ROWS[h]]
        return remote(ref, ref, so_out.at[l, h], so_in.at[l, h], sibling)

    def on(l, h, d, src, dz, src_z):
        ref = panels[l].at[core, src, src_z, ROWS[h]]
        peer = y_peer(d) if (d, dz) in ALONG_Y else z_peer(dz)
        return remote(ref, ref, on_out.at[l, h, dz, d], on_in.at[l, h, dz, d], peer)

    def sib(l, d, src, dz, src_z, side):
        ref = panels[l].at[side, src, src_z]
        return remote(ref, ref, s_out.at[l, dz, d], s_in.at[l, dz, d], sibling)

    def part(l, k, dst):
        src, to = parts.at[l, k], inbox.at[l, k]
        return remote(src, to, r_out.at[l, k], r_in.at[l, k], (row, dst))

    def send_own(l, h):
        for axis, d in OWN_ORDER:
            (yo(l, h, d, y) if axis == "y" else zo(l, h, d, z)).start()
        so(l, h, core).start()

    def gather(l):
        def y_arrival(d, h):
            yo(l, h, d, back(d)).wait_recv()
            for dz in (2, 1, 3):
                if (d, dz) not in ALONG_Y:
                    on(l, h, d, back(d), dz, z).start()
            if h == len(ROWS) - 1:
                sib(l, d, back(d), 0, z, core).start()

        def z_arrival(dz, h):
            zo(l, h, dz, back_z(dz)).wait_recv()
            for d in (4, 3, 5, 2, 6, 1, 7):
                if (d, dz) in ALONG_Y:
                    on(l, h, d, y, dz, back_z(dz)).start()
            if h == len(ROWS) - 1:
                sib(l, 0, y, dz, back_z(dz), core).start()

        for h in range(len(ROWS)):
            for axis, d in ARRIVAL_ORDER:
                (y_arrival if axis == "y" else z_arrival)(d, h)
        for d, dz in LAST_ORDER:
            for h in range(len(ROWS)):
                on(l, h, d, back(d), dz, back_z(dz)).wait_recv()
            sib(l, d, back(d), dz, back_z(dz), core).start()
        for h in range(len(ROWS)):
            so(l, h, 1 - core).wait_recv()
        for dz in range(NZ):
            for d in range(NY):
                if d or dz:
                    sib(l, d, back(d), dz, back_z(dz), 1 - core).wait_recv()

    def gather_sent(l):
        for h in range(len(ROWS)):
            so(l, h, core).wait_send()
            for d in range(1, NY):
                yo(l, h, d, y).wait_send()
            for dz in range(1, NZ):
                zo(l, h, dz, z).wait_send()
        for dz in range(NZ):
            for d in range(NY):
                if d and dz:
                    for h in range(len(ROWS)):
                        on(l, h, d, y, dz, z).wait_send()
                if d or dz:
                    sib(l, d, y, dz, z, core).wait_send()

    def products(l):
        def tile_step(t, _):
            block = panels[l][place[0, t], place[1, t], place[2, t]]
            product = jnp.dot(tiles[t], block, preferred_element_type=jnp.float32)
            runs[t] = runs[before[t]] + product
            return 0

        lax.fori_loop(0, slots, tile_step, 0, unroll=32)
        for k in range(1, reps):
            dst = lax.rem(rep + k, reps)
            parts[l, k] = runs[ends[dst]].astype(jnp.bfloat16)
            part(l, k, dst).start()

    def mix(l):
        total = runs[ends[rep]]
        for k in range(1, reps):
            part(l, k, rep).wait_recv()
            total += inbox[l, k].astype(jnp.float32)
        mixed = jnp.dot(
            total.astype(jnp.bfloat16), weights[l], preferred_element_type=jnp.float32
        )
        return jnp.maximum(mixed + biases[pl.ds(l, 1), :], 0.0).astype(jnp.bfloat16)

    layers = len(panels)
    for h in range(len(ROWS)):
        send_own(0, h)
    runs[...] = jnp.zeros_like(runs)
    link_slots()
    for l in range(layers):
        gather(l)
        if l == 0:
            for load in loads[3:]:
                load.wait()
        products(l)
        gather_sent(l)
        result = mix(l)
        if l + 1 < layers:
            panels[l + 1][core, y, z] = result
            for h in range(len(ROWS)):
                send_own(l + 1, h)
        else:
            out_ref[0] = result
    for l in range(layers):
        for k in range(1, reps):
            part(l, k, rep).wait_send()


def shards(features, tile_values, tile_rows, tile_cols, tile_count, weights, biases):
    slots = tile_values.shape[0]
    layers = weights.shape[0]
    reps = lax.axis_size("rep")
    smem = pl.BlockSpec(memory_space=pltpu.SMEM)
    hbm = pl.BlockSpec(memory_space=pl.ANY)
    dma = pltpu.SemaphoreType.DMA
    panel = pltpu.VMEM((NC, NY, NZ, SIDE, SIDE), jnp.bfloat16)
    return pl.pallas_call(
        layers_kernel,
        out_shape=jax.ShapeDtypeStruct(features.shape, jnp.bfloat16),
        in_specs=[hbm, hbm, smem, hbm, hbm, hbm, hbm],
        out_specs=pl.BlockSpec(memory_space=pltpu.VMEM),
        scratch_shapes=[
            pltpu.SMEM((slots,), jnp.int32),
            pltpu.SMEM((slots,), jnp.int32),
            pltpu.SMEM((3, slots), jnp.int32),
            pltpu.SMEM((slots,), jnp.int32),
            pltpu.SMEM((GROUPS,), jnp.int32),
            pltpu.VMEM((slots, SIDE, SIDE), jnp.bfloat16),
            pltpu.VMEM(weights.shape, jnp.bfloat16),
            pltpu.VMEM(biases.shape, jnp.float32),
            panel,
            panel,
            panel,
            pltpu.VMEM((slots + 1, SIDE, SIDE), jnp.float32),
            pltpu.VMEM((layers, reps, SIDE, SIDE), jnp.bfloat16),
            pltpu.VMEM((layers, reps, SIDE, SIDE), jnp.bfloat16),
            dma((6,)),
            dma((layers, len(ROWS), NZ)),
            dma((layers, len(ROWS), NZ)),
            dma((layers, len(ROWS), NY)),
            dma((layers, len(ROWS), NY)),
            dma((layers, len(ROWS), NZ, NY)),
            dma((layers, len(ROWS), NZ, NY)),
            dma((layers, len(ROWS))),
            dma((layers, len(ROWS))),
            dma((layers, NZ, NY)),
            dma((layers, NZ, NY)),
            dma((layers, reps)),
            dma((layers, reps)),
        ],
        compiler_params=pltpu.CompilerParams(
            collective_id=0, has_side_effects=True, vmem_limit_bytes=62 << 20
        ),
        name="layers",
    )(tile_rows, tile_cols, tile_count, features, tile_values, weights, biases)


def solution(mesh):
    in_specs = (
        P(("row", "rep"), None, None),
        P(("row", "rep"), None, None),
        P(("row", "rep")),
        P(("row", "rep")),
        P(("row", "rep")),
        P(),
        P(),
    )
    out_specs = P(("row", "rep"), None, None)
    return jax.shard_map(shards, mesh=mesh, in_specs=in_specs, out_specs=out_specs, check_vma=False)
```
